32 devices in a mesh: src: 2 (over z_hi), lat: 8 (over y, x, core), sub: 2 (over z_lo).
Axes of the slice: x: 2, y: 2, z: 4 (z_hi: 2, z_lo: 2; z = z_hi * 2 + z_lo), core: 2. Of those that a mesh axis runs over, the one named last changes fastest.
Arguments:
- sources: float32 [2, 24, 96, 2, 128], P(None, None, ('lat', 'sub'), 'src'), may hold values from -6 to 6
- eigvecs: bfloat16 [32, 24, 96, 2, 128], P(None, None, ('lat', 'sub'), 'src'), may hold values from -6 to 6
- eigvals: float32 [32], replicated, may hold values from 0.5 to 8
- links: float32 [4, 18, 96, 2, 128], P(None, None, ('lat', 'sub')), may hold values from -6 to 6
- damping: float32 [2], P('src'), may hold values from 0.5 to 1
Outputs:
- guess: float32 [2, 24, 96, 2, 128], P(None, None, ('lat', 'sub'), 'src')
- solution: float32 [2, 24, 96, 2, 128], P(None, None, ('lat', 'sub'), 'src')
The draws below stay inside these ranges and needn't reach their ends.
All inputs are finite; a program needn't handle non-finite values.
Results may differ from the reference program's by a relative error of at most 0.0047.
Values sent between devices are 32-bit elements; how exact they have to be, the bound alone decides.
A program may use at most 64 MiB of HBM per device.

```python
import math
import jax
import jax.numpy as jnp
import numpy as np
from jax import lax

LX = 16
LY = 8
NEV = 32
ITERS = 2
LZ = 2
TIME = 96
PLANE = 128
SOURCES = 2


def levels(stream_key, shape, pieces, low, top_value):
    gain, own = 1.0, jax.random.fold_in(stream_key, 6)
    for dim, parts in pieces:
        heights = jnp.exp(jax.random.uniform(jax.random.fold_in(own, dim), (parts,), jnp.float32, low / len(pieces), top_value / len(pieces)))
        gain = gain * jnp.repeat(heights, shape[dim] // parts).reshape([-1 if axis == dim else 1 for axis in range(len(shape))])
    return gain


def bell_draw(key, shape, deviation, reach, pieces=(), held_as=jnp.bfloat16):
    result = jax.random.normal(key, shape, jnp.float32) * deviation
    if len(pieces) > 0:
        result = levels(key, shape, pieces, -0.22, 0.18) * result
    return jnp.clip(result, min=-reach, max=reach).astype(held_as)


def setup_inputs(seed: int = 0) -> dict:
    arg_keys = jax.random.split(jax.random.key(seed), 6)
    return {
        "sources": bell_draw(arg_keys[0], (SOURCES, 24, TIME, LZ, PLANE), 1.0, 6.0, ((2, 16), (3, 2)), jnp.float32),
        "eigvecs": bell_draw(arg_keys[1], (NEV, 24, TIME, LZ, PLANE), 1.0, 6.0, ((2, 16), (3, 2))),
        "eigvals": jnp.clip(jnp.exp(jax.random.uniform(arg_keys[2], (NEV,), jnp.float32, math.log(0.5), math.log(8.0))), 0.5, 8.0),
        "links": bell_draw(arg_keys[3], (4, 18, TIME, LZ, PLANE), 0.4, 6.0, ((2, 16),), jnp.float32),
        "damping": jnp.clip(0.5 + 0.5 * jax.random.uniform(arg_keys[4], (SOURCES,), jnp.float32) ** levels(arg_keys[4], (SOURCES,), ((0, 2),), -0.2, 0.2), 0.5, 1.0),
    }


HOPPING = 0.12
PRECISE = lax.Precision.HIGHEST
SPIN_BLOCKS = [(np.array([[0.0, 0.0], [0.0, 0.0]]), np.array([[0.0, 1.0], [1.0, 0.0]])), (np.array([[0.0, -1.0], [1.0, 0.0]]), np.zeros((2, 2))), (np.array([[0.0, 0.0], [0.0, 0.0]]), np.array([[1.0, 0.0], [0.0, -1.0]])), (np.eye(2), np.zeros((2, 2)))]

def spin_apply(table_re, table_im, real_part, imag_part):
    matrix_re = jnp.asarray(table_re, jnp.float32)
    matrix_im = jnp.asarray(table_im, jnp.float32)

    def product(matrix, values):
        return jnp.einsum('pq,sq...->sp...', matrix, values, precision=PRECISE)
    return (product(matrix_re, real_part) - product(matrix_im, imag_part), product(matrix_re, imag_part) + product(matrix_im, real_part))

def project(sign, direction, real_part, imag_part):
    table_re, table_im = SPIN_BLOCKS[direction]
    lower_re, lower_im = spin_apply(table_re, table_im, real_part[:, 2:], imag_part[:, 2:])
    return (real_part[:, :2] + sign * lower_re, imag_part[:, :2] + sign * lower_im)

def rebuild(sign, direction, upper_re, upper_im):
    table_re, table_im = SPIN_BLOCKS[direction]
    lower_re, lower_im = spin_apply(table_re.T, -table_im.T, upper_re, upper_im)
    return (jnp.concatenate([upper_re, sign * lower_re], 1), jnp.concatenate([upper_im, sign * lower_im], 1))

def color_mul(links_re, links_im, real_part, imag_part):

    def product(table, values):
        return jnp.einsum('actzw,sbctzw->sbatzw', table, values, precision=PRECISE)
    return (product(links_re, real_part) - product(links_im, imag_part), product(links_re, imag_part) + product(links_im, real_part))

def color_adj(links_re, links_im, real_part, imag_part):

    def product(table, values):
        return jnp.einsum('catzw,sbctzw->sbatzw', table, values, precision=PRECISE)
    return (product(links_re, real_part) + product(links_im, imag_part), product(links_re, imag_part) - product(links_im, real_part))

def link_parts(links, direction):
    extent = links.shape[2:]
    return (links[direction, :9].reshape((3, 3) + extent), links[direction, 9:].reshape((3, 3) + extent))

def neighbour(values, direction, step, antiperiodic):
    if direction == 0:
        shaped = values.reshape(values.shape[:-1] + (LY, LX))
        return jnp.roll(shaped, -step, axis=-1).reshape(values.shape)
    if direction == 1:
        shaped = values.reshape(values.shape[:-1] + (LY, LX))
        return jnp.roll(shaped, -step, axis=-2).reshape(values.shape)
    if direction == 2:
        return jnp.roll(values, -step, axis=-2)
    moved = jnp.roll(values, -step, axis=-3)
    if antiperiodic:
        length = values.shape[-3]
        edge = length - 1 if step > 0 else 0
        factor = jnp.where(jnp.arange(length) == edge, -1.0, 1.0).astype(jnp.float32)
        moved = moved * factor[:, None, None]
    return moved

def split_parts(spinor):
    count = spinor.shape[0]
    extent = spinor.shape[2:]
    return (spinor[:, :12].reshape((count, 4, 3) + extent), spinor[:, 12:].reshape((count, 4, 3) + extent))

def join_parts(real_part, imag_part):
    count = real_part.shape[0]
    extent = real_part.shape[3:]
    return jnp.concatenate([real_part.reshape((count, 12) + extent), imag_part.reshape((count, 12) + extent)], 1)

def wilson(spinor, links):
    real_part, imag_part = split_parts(spinor)
    terms = []
    for direction in range(4):
        links_re, links_im = link_parts(links, direction)
        ahead_re = neighbour(real_part, direction, 1, True)
        ahead_im = neighbour(imag_part, direction, 1, True)
        carried = color_mul(links_re, links_im, ahead_re, ahead_im)
        terms.append(rebuild(-1.0, direction, *project(-1.0, direction, *carried)))
        back_re = neighbour(links_re, direction, -1, False)
        back_im = neighbour(links_im, direction, -1, False)
        behind_re = neighbour(real_part, direction, -1, True)
        behind_im = neighbour(imag_part, direction, -1, True)
        carried = color_adj(back_re, back_im, behind_re, behind_im)
        terms.append(rebuild(1.0, direction, *project(1.0, direction, *carried)))
    total_re, total_im = terms[0]
    for extra in terms[1:]:
        total_re = total_re + extra[0]
        total_im = total_im + extra[1]
    return spinor - HOPPING * join_parts(total_re, total_im)

def reference(sources, eigvecs, eigvals, links, damping):
    count = sources.shape[0]
    flat_src = sources.astype(jnp.bfloat16).reshape(count, 24, -1)
    swapped = jnp.concatenate([flat_src[:, 12:], -flat_src[:, :12]], 1)
    stacked = jnp.concatenate([flat_src, swapped], 0).reshape(2 * count, -1)
    flat_vec = eigvecs.reshape(eigvecs.shape[0], -1)
    correlation = lax.dot_general(flat_vec, stacked, (((1,), (1,)), ((), ())), preferred_element_type=jnp.float32)
    correlation = correlation / math.sqrt(24 * (flat_vec.shape[1] // 24))
    weights = jnp.concatenate([correlation[:, :count].T, correlation[:, count:].T], 0) / eigvals[None, :]
    weights = weights.astype(jnp.bfloat16)
    mixed = jnp.dot(weights, flat_vec, preferred_element_type=jnp.float32)
    middle = mixed.shape[1] // 2
    guess = jnp.concatenate([mixed[:count, :middle] - mixed[count:, middle:], mixed[:count, middle:] + mixed[count:, :middle]], 1).reshape(sources.shape)

    def solve(item):
        source, start, rate = item
        source = source[None]
        iterate = start[None]
        for sweep in range(ITERS):
            iterate = iterate + rate * (source - wilson(iterate, links))
        return iterate[0]
    solution = lax.map(solve, (sources, guess, damping))
    return (guess, solution)
```

```python
import functools
import math

import jax
import jax.numpy as jnp
from jax import lax
from jax.experimental import pallas as pl
from jax.experimental.pallas import tpu as pltpu
from jax.sharding import PartitionSpec as P

LX = 16
HOPPING = 0.12
MESH = pl.DeviceIdType.MESH

BLOCKS = [((1, 1), (0, 1)), ((1, 2), (0, 0)), ((0, 1), (1, 3)), ((0, 0), (1, 0))]
BLOCKS_H = [((1, 3), (0, 3)), ((1, 0), (0, 2)), ((0, 3), (1, 1)), ((0, 0), (1, 0))]


def add_phase(a, b, power):
    power %= 4
    if power == 0:
        return a[0] + b[0], a[1] + b[1]
    if power == 1:
        return a[0] - b[1], a[1] + b[0]
    if power == 2:
        return a[0] - b[0], a[1] - b[1]
    return a[0] + b[1], a[1] - b[0]


def project(sign, d, x):
    turn = 0 if sign > 0 else 2
    return [add_phase(x[r], x[2 + BLOCKS[d][r][0]], BLOCKS[d][r][1] + turn) for r in range(2)]


def rebuild(sign, d, half, acc):
    turn = 0 if sign > 0 else 2
    out = [add_phase(acc[r], half[r], 0) for r in range(2)]
    for r in range(2):
        col, power = BLOCKS_H[d][r]
        out.append(add_phase(acc[2 + r], half[col], power + turn))
    return out


def color_mul(u, half):
    ur, ui = u
    out = []
    for hr, hi in half:
        re = im = None
        for c in range(3):
            a, b = ur[:, c], ui[:, c]
            x, y = hr[c][None], hi[c][None]
            tr, ti = a * x - b * y, a * y + b * x
            re, im = (tr, ti) if re is None else (re + tr, im + ti)
        out.append((re, im))
    return out


def color_adj(u, half):
    ur, ui = u
    out = []
    for hr, hi in half:
        re = im = None
        for c in range(3):
            a, b = ur[c], ui[c]
            x, y = hr[c][None], hi[c][None]
            tr, ti = a * x + b * y, a * y - b * x
            re, im = (tr, ti) if re is None else (re + tr, im + ti)
        out.append((re, im))
    return out


def each(half, fn):
    return [(fn(re), fn(im)) for re, im in half]


def distinct(offsets, n):
    out = []
    for o in offsets:
        if o % n not in out:
            out.append(o % n)
    return out


def kernel(
    shape, sizes,
    src, eig, eigvals, links, damping, guess, sol,
    sa, sb, corr, slots, w2, xe0, xe1, sr, le, hs, gs, hr0, gr0, hr1, gr1, acc_ref,
    ar_send, ar_recv, sr_send, sr_recv, xe_send, xe_recv, h_send, h_recv, g_send, g_recv,
    h1_sem, g1_sem,
):
    T, LZ, S, K, TP = shape
    n, L, U = sizes
    N = n * L * U
    NT = L * U
    V = T * 24
    d0 = distinct((0, 1, -1, 2, -2), n)
    d1 = distinct((0, 1, -1), n)
    dl = distinct((0, 1, -1, -2), n)
    rows = 2 * S * K // 128
    me_s, me_l, me_u = lax.axis_index("src"), lax.axis_index("lat"), lax.axis_index("sub")
    place = me_l * U + me_u
    me = me_s * NT + place

    def device(s_index, t_index):
        return {"src": s_index, "lat": lax.div(t_index, U), "sub": lax.rem(t_index, U)}

    def of(g):
        return device(lax.div(g, NT), lax.rem(g, NT))

    above, below = lax.rem(place + 1, NT), lax.rem(place + NT - 1, NT)
    top_flip = jnp.where(place == NT - 1, -1.0, 1.0).astype(jnp.float32)
    bottom_flip = jnp.where(place == 0, -1.0, 1.0).astype(jnp.float32)

    barrier = pltpu.get_barrier_semaphore()

    def greet(i, carry):
        pl.semaphore_signal(barrier, inc=1, device_id=of(lax.rem(me + i, N)), device_id_type=MESH)
        return carry

    lax.fori_loop(1, N, greet, 0)

    for s in range(S):
        for t in range(T):
            low = [
                src[pl.ds(s * V + p * 12 * T + t, 12, stride=T), :]
                .astype(jnp.bfloat16)
                .astype(jnp.float32)
                for p in range(2)
            ]
            sa[s, pl.ds(t * 24, 12), :] = low[0]
            sa[s, pl.ds(t * 24 + 12, 12), :] = low[1]
            sb[s, pl.ds(t * 24, 12), :] = low[1]
            sb[s, pl.ds(t * 24 + 12, 12), :] = -low[0]

    def correlate(k, carry):
        e = eig[k].astype(jnp.float32)
        for p, ref in enumerate((sa, sb)):
            for s in range(S):
                part = jnp.sum((e * ref[s]).reshape(V // 8, 8, 128), axis=0)
                corr[pl.ds((p * S + s) * K + k, 1), :] = jnp.sum(part, axis=0, keepdims=True)
        return carry

    lax.fori_loop(0, K, correlate, 0)
    flat = lax.dot_general(
        jnp.ones((8, 128), jnp.float32), corr[...], (((1,), (1,)), ((), ())),
        preferred_element_type=jnp.float32, precision=lax.Precision.HIGHEST,
    )
    for r in range(rows):
        slots[me, pl.ds(r, 1), :] = flat[0:1, r * 128 : (r + 1) * 128]
    slots[me, pl.ds(rows, 1), :] = jnp.full((1, 128), damping[0], jnp.float32)
    sr[0, pl.ds(0, S * V), :] = src[...]

    pl.semaphore_wait(barrier, N - 1)

    def spread(i, carry):
        pltpu.make_async_remote_copy(
            src_ref=slots.at[me], dst_ref=slots.at[me], send_sem=ar_send, recv_sem=ar_recv,
            device_id=of(lax.rem(me + i, N)), device_id_type=MESH,
        ).start()
        return carry

    lax.fori_loop(1, N, spread, 0)

    sent = []
    src_copies = {}
    for i, o in enumerate(d1):
        if o:
            copy = pltpu.make_async_remote_copy(
                src_ref=src, dst_ref=sr.at[i, pl.ds(0, S * V)],
                send_sem=sr_send.at[i], recv_sem=sr_recv.at[i],
                device_id=device(lax.rem(me_s + n - o, n), place), device_id_type=MESH,
            )
            copy.start()
            sent.append(copy)
            src_copies[i] = copy

    for i, o in enumerate(dl):
        z = lax.rem(me_s + o, n)

        def arrange(c, carry):
            le[i, c, pl.ds(0, T), :] = links[pl.ds(c * T * LZ + z, T, stride=LZ), :]
            return carry

        lax.fori_loop(0, 72, arrange, 0)

    every = slots.at[pl.ds(0, N - 1)]
    pltpu.make_async_copy(every, every, ar_recv).wait()
    total = jnp.sum(slots[...], axis=0)
    eye = lax.broadcasted_iota(jnp.int32, (128, 128), 0) == lax.broadcasted_iota(
        jnp.int32, (128, 128), 1
    )
    values = jnp.concatenate([eigvals[...]] * (128 // K), axis=1)
    scale = math.sqrt(24 * T * NT * LZ * 128)
    for r in range(rows):
        w = (total[r : r + 1] / scale / values).astype(jnp.bfloat16).astype(jnp.float32)
        w2[pl.ds(r * 128, 128), :] = jnp.dot(
            jnp.where(eye, w, 0.0).astype(jnp.bfloat16), jnp.ones((128, 128), jnp.bfloat16),
            preferred_element_type=jnp.float32,
        )

    def tile(ref, index):
        parts = [
            [
                jnp.stack([ref[index, pl.ds(p * 12 + sp * 3 + c, TP, stride=24), :] for c in range(3)])
                for sp in range(4)
            ]
            for p in range(2)
        ]
        return [(parts[0][sp], parts[1][sp]) for sp in range(4)]

    def link(o, d):
        i = dl.index(o % n)
        return (
            le[i, pl.ds(d * 18, 9)].reshape(3, 3, TP, 128),
            le[i, pl.ds(d * 18 + 9, 9)].reshape(3, 3, TP, 128),
        )

    def put_halo(buf, s, half, row):
        for p in range(2):
            for sp in range(2):
                buf[s, pl.ds(p * 6 + sp * 3, 3)] = half[sp][p][:, row : row + 1, :]

    def get_halo(buf, index, flip):
        return [
            tuple(buf[index, pl.ds(p * 6 + sp * 3, 3)] * flip for p in range(2)) for sp in range(2)
        ]

    def edges_all(ref, j):
        def body(s, carry):
            x = tile(ref, s)
            put_halo(hs.at[j], s, project(-1, 3, x), 0)
            put_halo(gs.at[j], s, color_adj(link(0, 3), project(1, 3, x)), T - 1)
            return carry

        lax.fori_loop(0, S, body, 0)

    def send_halo(buf, dest, send, recv, t_index, offsets):
        out = []
        for i, o in enumerate(offsets):
            copy = pltpu.make_async_remote_copy(
                src_ref=buf, dst_ref=dest.at[pl.ds(i * S, S)], send_sem=send.at[i],
                recv_sem=recv.at[i], device_id=device(lax.rem(me_s + n - o, n), t_index),
                device_id_type=MESH,
            )
            copy.start()
            out.append(copy)
        return out

    step = 48 if T % 2 == 0 else V
    chunks = list(range(V // step))
    order = [chunks[0]] + chunks[-1:0:-1]
    xe_copies = []
    h_copies = g_copies = None
    for done, ch in enumerate(order):

        def mix(k, acc):
            e = eig[k, pl.ds(ch * step, step), :].astype(jnp.float32)
            return tuple(
                a + w2[pl.ds(j * K + k, 1), :] * e for j, a in enumerate(acc)
            )

        acc = lax.fori_loop(
            0, K, mix, tuple(jnp.zeros((step, 128), jnp.float32) for _ in range(2 * S)), unroll=4
        )
        for s in range(S):
            one, two = acc[s], acc[S + s]
            for t in range(step // 24):
                b = t * 24
                turned = jnp.concatenate([-two[b + 12 : b + 24], two[b : b + 12]], axis=0)
                xe0[s, pl.ds(ch * step + b, 24), :] = one[b : b + 24] + turned
        if done == min(1, len(order) - 1):
            edges_all(xe0, 0)
            h_copies = send_halo(hs.at[0], hr0, h_send, h_recv, below, d1)
            g_copies = send_halo(gs.at[0], gr0, g_send, g_recv, above, d1)
        for i, o in enumerate(d0):
            if o:
                part = pl.ds(ch * step, step)
                copy = pltpu.make_async_remote_copy(
                    src_ref=xe0.at[pl.ds(0, S), part], dst_ref=xe0.at[pl.ds(i * S, S), part],
                    send_sem=xe_send.at[i, ch], recv_sem=xe_recv.at[i, ch],
                    device_id=device(lax.rem(me_s + n - o, n), place), device_id_type=MESH,
                )
                copy.start()
                xe_copies.append(copy)
    for s in range(S):
        for c in range(24):
            guess[pl.ds((s * 24 + c) * T, T), :] = xe0[s, pl.ds(c, T, stride=24), :]

    row = lax.broadcasted_iota(jnp.int32, (1, TP, 128), 1)
    column = lax.rem(lax.broadcasted_iota(jnp.int32, (1, TP, 128), 2), LX)

    def shift(v, d, by):
        if d == 0:
            border = LX - 1 if by > 0 else 0
            inside = pltpu.roll(v, (-by) % 128, 2)
            wrapped = pltpu.roll(v, (by * (LX - 1)) % 128, 2)
            return jnp.where(column == border, wrapped, inside)
        return pltpu.roll(v, (-by * LX) % 128, 2)

    def plane_hops(x, o, acc):
        for d in range(2):
            u = link(o, d)
            ahead = each(project(-1, d, x), lambda v: shift(v, d, 1))
            acc = rebuild(-1, d, color_mul(u, ahead), acc)
            behind = each(color_adj(u, project(1, d, x)), lambda v: shift(v, d, -1))
            acc = rebuild(1, d, behind, acc)
        return acc

    def z_hops(ahead, behind, o, acc):
        acc = rebuild(-1, 2, color_mul(link(o, 2), project(-1, 2, ahead)), acc)
        return rebuild(1, 2, color_adj(link(o - 1, 2), project(1, 2, behind)), acc)

    def t_hops(x, o, hbuf, gbuf, index, acc):
        u = link(o, 3)

        def joined(half, halo, by, at):
            return [
                tuple(
                    jnp.where(row == at, jnp.broadcast_to(q, (3, TP, 128)), pltpu.roll(v, by % TP, 1))
                    for v, q in zip(hv, qv)
                )
                for hv, qv in zip(half, halo)
            ]

        ahead = joined(project(-1, 3, x), get_halo(hbuf, index, top_flip), -1, T - 1)
        acc = rebuild(-1, 3, color_mul(u, ahead), acc)
        behind = joined(
            color_adj(u, project(1, 3, x)), get_halo(gbuf, index, bottom_flip), 1, 0
        )
        return rebuild(1, 3, behind, acc)

    zero = [(jnp.zeros((3, TP, 128), jnp.float32),) * 2] * 4

    def keep(s, acc):
        for sp in range(4):
            for p in range(2):
                acc_ref[s, pl.ds(p * 12 + sp * 3, 3)] = acc[sp][p]

    def kept(s):
        return [
            tuple(acc_ref[s, pl.ds(p * 12 + sp * 3, 3)] for p in range(2)) for sp in range(4)
        ]

    def updated(x, acc, i, s, write):
        rate = slots[s * NT, pl.ds(rows, 1), :]
        for sp in range(4):
            for p in range(2):
                for c in range(3):
                    comp = p * 12 + sp * 3 + c
                    b = sr[i, pl.ds((s * 24 + comp) * T, TP), :]
                    v = x[sp][p][c]
                    write(comp, v + rate * (b - (v - HOPPING * acc[sp][p][c])))

    def slot(offsets, o, s):
        return offsets.index(o % n) * S + s

    def loop(body):
        def step_body(s, carry):
            body(s)
            return carry

        lax.fori_loop(0, S, step_body, 0)

    loop(lambda s: keep(s, plane_hops(tile(xe0, s), 0, zero)))
    for copy in h_copies + g_copies:
        copy.wait_recv()
    loop(lambda s: keep(s, t_hops(tile(xe0, s), 0, hr0, gr0, s, kept(s))))
    for copy in xe_copies:
        copy.wait_recv()
    def first(i, o, s):
        x = tile(xe0, slot(d0, o, s))
        acc = kept(s) if i == 0 else plane_hops(x, o, zero)
        if i:
            acc = t_hops(x, o, hr0, gr0, i * S + s, acc)
        acc = z_hops(tile(xe0, slot(d0, o + 1, s)), tile(xe0, slot(d0, o - 1, s)), o, acc)

        def write(comp, v):
            xe1[i * S + s, pl.ds(comp, TP, stride=24), :] = v

        updated(x, acc, i, s, write)

    loop(lambda s: first(0, 0, s))

    edges_all(xe1, 1)
    h_next = send_halo(hs.at[1], hr1, h1_sem.at[0], h1_sem.at[1], below, [0])
    g_next = send_halo(gs.at[1], gr1, g1_sem.at[0], g1_sem.at[1], above, [0])
    for i in src_copies:
        src_copies[i].wait_recv()
    for i, o in enumerate(d1):
        if o:
            loop(lambda s: first(i, o, s))

    def inner(s):
        x = tile(xe1, s)
        acc = plane_hops(x, 0, zero)
        keep(s, z_hops(tile(xe1, slot(d1, 1, s)), tile(xe1, slot(d1, -1, s)), 0, acc))

    loop(inner)
    for copy in h_next + g_next:
        copy.wait_recv()

    def last(s):
        x = tile(xe1, s)
        acc = t_hops(x, 0, hr1, gr1, s, kept(s))

        def write(comp, v):
            sol[pl.ds((s * 24 + comp) * T, T), :] = v[0:T]

        updated(x, acc, 0, s, write)

    loop(last)
    for copy in sent + xe_copies + h_copies + g_copies + h_next + g_next:
        copy.wait_send()
    pltpu.make_async_copy(every, every, ar_send).wait()


def solution(mesh):
    n, L, U = mesh.shape["src"], mesh.shape["lat"], mesh.shape["sub"]

    def shards(sources, eigvecs, eigvals, links, damping):
        S, _, T, _, _ = sources.shape
        K, LZ = eigvecs.shape[0], links.shape[3]
        TP = -(-T // 8) * 8
        V = T * 24
        N = n * L * U
        rows = 2 * S * K // 128
        d0 = len(distinct((0, 1, -1, 2, -2), n))
        d1 = len(distinct((0, 1, -1), n))
        dl = len(distinct((0, 1, -1, -2), n))
        vmem = pl.BlockSpec(memory_space=pltpu.VMEM)
        smem = pl.BlockSpec(memory_space=pltpu.SMEM)
        f32 = jnp.float32
        dma = pltpu.SemaphoreType.DMA
        chunks = T // 2 if T % 2 == 0 else 1
        guess, result = pl.pallas_call(
            functools.partial(kernel, (T, LZ, S, K, TP), (n, L, U)),
            out_shape=[jax.ShapeDtypeStruct((S * V, 128), f32)] * 2,
            in_specs=[vmem, vmem, vmem, vmem, smem],
            out_specs=[vmem, vmem],
            scratch_shapes=[
                pltpu.VMEM((S, V, 128), f32),
                pltpu.VMEM((S, V, 128), f32),
                pltpu.VMEM((2 * S * K, 128), f32),
                pltpu.VMEM((N, rows + 1, 128), f32),
                pltpu.VMEM((2 * S * K, 128), f32),
                pltpu.VMEM((d0 * S, TP * 24, 128), f32),
                pltpu.VMEM((d1 * S, TP * 24, 128), f32),
                pltpu.VMEM((d1, S * V + 8, 128), f32),
                pltpu.VMEM((dl, 72, TP, 128), f32),
                pltpu.VMEM((2, S, 12, 1, 128), f32),
                pltpu.VMEM((2, S, 12, 1, 128), f32),
                pltpu.VMEM((d1 * S, 12, 1, 128), f32),
                pltpu.VMEM((d1 * S, 12, 1, 128), f32),
                pltpu.VMEM((S, 12, 1, 128), f32),
                pltpu.VMEM((S, 12, 1, 128), f32),
                pltpu.VMEM((S, 24, TP, 128), f32),
                dma, dma, dma((d1,)), dma((d1,)), dma((d0, chunks)), dma((d0, chunks)),
                dma((d1,)), dma((d1,)), dma((d1,)), dma((d1,)), dma((2, 1)), dma((2, 1)),
            ],
            compiler_params=pltpu.CompilerParams(
                collective_id=0, has_side_effects=True, vmem_limit_bytes=40 * 1024 * 1024
            ),
        )(
            sources.reshape(S * V, 128),
            eigvecs.transpose(0, 2, 3, 1, 4).reshape(K, V, 128),
            eigvals.reshape(1, K),
            links.reshape(72 * T * LZ, 128),
            damping,
        )
        return guess.reshape(sources.shape), result.reshape(sources.shape)

    spread = P(None, None, ("lat", "sub"), "src", None)
    return jax.shard_map(
        shards,
        mesh=mesh,
        in_specs=(spread, spread, P(), P(None, None, ("lat", "sub"), None, None), P("src")),
        out_specs=(spread, spread),
        check_vma=False,
    )
```

```python
import functools
import math

import jax
import jax.numpy as jnp
from jax import lax
from jax.experimental import pallas as pl
from jax.experimental.pallas import tpu as pltpu
from jax.sharding import PartitionSpec as P

LX = 16
EIG_BLOCK = 8
HOPPING = 0.12
MESH = pl.DeviceIdType.MESH

BLOCKS = [((1, 1), (0, 1)), ((1, 2), (0, 0)), ((0, 1), (1, 3)), ((0, 0), (1, 0))]
BLOCKS_H = [((1, 3), (0, 3)), ((1, 0), (0, 2)), ((0, 3), (1, 1)), ((0, 0), (1, 0))]


def add_phase(a, b, power):
    power %= 4
    if power == 0:
        return a[0] + b[0], a[1] + b[1]
    if power == 1:
        return a[0] - b[1], a[1] + b[0]
    if power == 2:
        return a[0] - b[0], a[1] - b[1]
    return a[0] + b[1], a[1] - b[0]


def project(sign, d, x):
    turn = 0 if sign > 0 else 2
    return [add_phase(x[r], x[2 + BLOCKS[d][r][0]], BLOCKS[d][r][1] + turn) for r in range(2)]


def rebuild(sign, d, half, acc):
    turn = 0 if sign > 0 else 2
    out = [add_phase(acc[r], half[r], 0) for r in range(2)]
    for r in range(2):
        col, power = BLOCKS_H[d][r]
        out.append(add_phase(acc[2 + r], half[col], power + turn))
    return out


def color_mul(u, half):
    ur, ui = u
    out = []
    for hr, hi in half:
        re = im = None
        for c in range(3):
            a, b = ur[:, c], ui[:, c]
            x, y = hr[c][None], hi[c][None]
            tr, ti = a * x - b * y, a * y + b * x
            re, im = (tr, ti) if re is None else (re + tr, im + ti)
        out.append((re, im))
    return out


def color_adj(u, half):
    ur, ui = u
    out = []
    for hr, hi in half:
        re = im = None
        for c in range(3):
            a, b = ur[c], ui[c]
            x, y = hr[c][None], hi[c][None]
            tr, ti = a * x + b * y, a * y - b * x
            re, im = (tr, ti) if re is None else (re + tr, im + ti)
        out.append((re, im))
    return out


def each(half, fn):
    return [(fn(re), fn(im)) for re, im in half]


def distinct(offsets, n):
    out = []
    for o in offsets:
        if o % n not in out:
            out.append(o % n)
    return out


def kernel(
    shape, sizes,
    src_hbm, eig_hbm, eigvals_hbm, links_hbm, damping_hbm, guess, sol,
    src, eig, eigvals, links, damping, in_sem, eig_sem,
    sa, sb, corr, slots, w2, xe0, xe1, sr, le, hs, gs, hr0, gr0, hr1, gr1, acc_ref,
    ar_send, ar_recv, sr_send, sr_recv, xe_send, xe_recv, h_send, h_recv, g_send, g_recv,
    h1_sem, g1_sem,
):
    T, LZ, S, K, TP = shape
    n, L, U = sizes
    N = n * L * U
    NT = L * U
    V = T * 24
    d0 = distinct((0, 1, -1, 2, -2), n)
    d1 = distinct((0, 1, -1), n)
    dl = distinct((0, 1, -1, -2), n)
    rows = 2 * S * K // 128
    me_s, me_l, me_u = lax.axis_index("src"), lax.axis_index("lat"), lax.axis_index("sub")
    place = me_l * U + me_u
    me = me_s * NT + place

    def device(s_index, t_index):
        return {"src": s_index, "lat": lax.div(t_index, U), "sub": lax.rem(t_index, U)}

    def of(g):
        return device(lax.div(g, NT), lax.rem(g, NT))

    above, below = lax.rem(place + 1, NT), lax.rem(place + NT - 1, NT)
    top_flip = jnp.where(place == NT - 1, -1.0, 1.0).astype(jnp.float32)
    bottom_flip = jnp.where(place == 0, -1.0, 1.0).astype(jnp.float32)

    barrier = pltpu.get_barrier_semaphore()

    def greet(i, carry):
        pl.semaphore_signal(barrier, inc=1, device_id=of(lax.rem(me + i, N)), device_id_type=MESH)
        return carry

    parts = K // EIG_BLOCK
    loads = [
        pltpu.make_async_copy(a, b, in_sem.at[i])
        for i, (a, b) in enumerate(
            [(src_hbm, src), (damping_hbm, damping), (eigvals_hbm, eigvals), (links_hbm, links)]
        )
    ]
    eig_loads = [
        pltpu.make_async_copy(
            eig_hbm.at[pl.ds(j * EIG_BLOCK, EIG_BLOCK)], eig.at[pl.ds(j * EIG_BLOCK, EIG_BLOCK)],
            eig_sem.at[j],
        )
        for j in range(parts)
    ]
    loads[0].start()
    lax.fori_loop(1, N, greet, 0)
    for copy in eig_loads + loads[1:]:
        copy.start()
    loads[0].wait()

    for s in range(S):
        for t in range(T):
            low = [
                src[pl.ds(s * V + p * 12 * T + t, 12, stride=T), :]
                .astype(jnp.bfloat16)
                .astype(jnp.float32)
                for p in range(2)
            ]
            sa[s, pl.ds(t * 24, 12), :] = low[0]
            sa[s, pl.ds(t * 24 + 12, 12), :] = low[1]
            sb[s, pl.ds(t * 24, 12), :] = low[1]
            sb[s, pl.ds(t * 24 + 12, 12), :] = -low[0]

    def correlate(k, carry):
        e = eig[k].astype(jnp.float32)
        for p, ref in enumerate((sa, sb)):
            for s in range(S):
                part = jnp.sum((e * ref[s]).reshape(V // 8, 8, 128), axis=0)
                corr[pl.ds((p * S + s) * K + k, 1), :] = jnp.sum(part, axis=0, keepdims=True)
        return carry

    sr[0, pl.ds(0, S * V), :] = src[...]
    sent = []
    src_copies = {}
    for j in range(parts):
        if j == parts // 2:
            pl.semaphore_wait(barrier, N - 1)
            for i, o in enumerate(d1):
                if o:
                    copy = pltpu.make_async_remote_copy(
                        src_ref=src, dst_ref=sr.at[i, pl.ds(0, S * V)],
                        send_sem=sr_send.at[i], recv_sem=sr_recv.at[i],
                        device_id=device(lax.rem(me_s + n - o, n), place), device_id_type=MESH,
                    )
                    copy.start()
                    sent.append(copy)
                    src_copies[i] = copy
        eig_loads[j].wait()
        lax.fori_loop(j * EIG_BLOCK, (j + 1) * EIG_BLOCK, correlate, 0)
    flat = lax.dot_general(
        jnp.ones((8, 128), jnp.float32), corr[...], (((1,), (1,)), ((), ())),
        preferred_element_type=jnp.float32, precision=lax.Precision.HIGHEST,
    )
    for r in range(rows):
        slots[me, pl.ds(r, 1), :] = flat[0:1, r * 128 : (r + 1) * 128]
    loads[1].wait()
    slots[me, pl.ds(rows, 1), :] = jnp.broadcast_to(damping[...], (1, 128))

    def spread(i, carry):
        pltpu.make_async_remote_copy(
            src_ref=slots.at[me], dst_ref=slots.at[me], send_sem=ar_send, recv_sem=ar_recv,
            device_id=of(lax.rem(me + i, N)), device_id_type=MESH,
        ).start()
        return carry

    lax.fori_loop(1, N, spread, 0)
    loads[2].wait()
    loads[3].wait()

    for i, o in enumerate(dl):
        z = lax.rem(me_s + o, n)

        def arrange(c, carry):
            le[i, c, pl.ds(0, T), :] = links[pl.ds(c * T * LZ + z, T, stride=LZ), :]
            return carry

        lax.fori_loop(0, 72, arrange, 0)

    every = slots.at[pl.ds(0, N - 1)]
    pltpu.make_async_copy(every, every, ar_recv).wait()
    total = jnp.sum(slots[...], axis=0)
    eye = lax.broadcasted_iota(jnp.int32, (128, 128), 0) == lax.broadcasted_iota(
        jnp.int32, (128, 128), 1
    )
    values = jnp.concatenate([eigvals[...]] * (128 // K), axis=1)
    scale = math.sqrt(24 * T * NT * LZ * 128)
    for r in range(rows):
        w = (total[r : r + 1] / scale / values).astype(jnp.bfloat16).astype(jnp.float32)
        w2[pl.ds(r * 128, 128), :] = jnp.dot(
            jnp.where(eye, w, 0.0).astype(jnp.bfloat16), jnp.ones((128, 128), jnp.bfloat16),
            preferred_element_type=jnp.float32,
        )

    def tile(ref, index):
        parts = [
            [
                jnp.stack([ref[index, pl.ds(p * 12 + sp * 3 + c, TP, stride=24), :] for c in range(3)])
                for sp in range(4)
            ]
            for p in range(2)
        ]
        return [(parts[0][sp], parts[1][sp]) for sp in range(4)]

    def link(o, d):
        i = dl.index(o % n)
        return (
            le[i, pl.ds(d * 18, 9)].reshape(3, 3, TP, 128),
            le[i, pl.ds(d * 18 + 9, 9)].reshape(3, 3, TP, 128),
        )

    def put_halo(buf, s, half, row):
        for p in range(2):
            for sp in range(2):
                buf[s, pl.ds(p * 6 + sp * 3, 3)] = half[sp][p][:, row : row + 1, :]

    def get_halo(buf, index, flip):
        return [
            tuple(buf[index, pl.ds(p * 6 + sp * 3, 3)] * flip for p in range(2)) for sp in range(2)
        ]

    def edges_all(ref, j):
        def body(s, carry):
            x = tile(ref, s)
            put_halo(hs.at[j], s, project(-1, 3, x), 0)
            put_halo(gs.at[j], s, color_adj(link(0, 3), project(1, 3, x)), T - 1)
            return carry

        lax.fori_loop(0, S, body, 0)

    def send_halo(buf, dest, send, recv, t_index, offsets):
        out = []
        for i, o in enumerate(offsets):
            copy = pltpu.make_async_remote_copy(
                src_ref=buf, dst_ref=dest.at[pl.ds(i * S, S)], send_sem=send.at[i],
                recv_sem=recv.at[i], device_id=device(lax.rem(me_s + n - o, n), t_index),
                device_id_type=MESH,
            )
            copy.start()
            out.append(copy)
        return out

    step = 48 if T % 2 == 0 else V
    chunks = list(range(V // step))
    order = [chunks[0]] + chunks[-1:0:-1]
    xe_copies = []
    h_copies = g_copies = None
    for done, ch in enumerate(order):

        def mix(k, acc):
            e = eig[k, pl.ds(ch * step, step), :].astype(jnp.float32)
            return tuple(
                a + w2[pl.ds(j * K + k, 1), :] * e for j, a in enumerate(acc)
            )

        acc = lax.fori_loop(
            0, K, mix, tuple(jnp.zeros((step, 128), jnp.float32) for _ in range(2 * S)), unroll=4
        )
        for s in range(S):
            one, two = acc[s], acc[S + s]
            for t in range(step // 24):
                b = t * 24
                turned = jnp.concatenate([-two[b + 12 : b + 24], two[b : b + 12]], axis=0)
                xe0[s, pl.ds(ch * step + b, 24), :] = one[b : b + 24] + turned
        if done == min(1, len(order) - 1):
            edges_all(xe0, 0)
            h_copies = send_halo(hs.at[0], hr0, h_send, h_recv, below, d1)
            g_copies = send_halo(gs.at[0], gr0, g_send, g_recv, above, d1)
        for i, o in enumerate(d0):
            if o:
                part = pl.ds(ch * step, step)
                copy = pltpu.make_async_remote_copy(
                    src_ref=xe0.at[pl.ds(0, S), part], dst_ref=xe0.at[pl.ds(i * S, S), part],
                    send_sem=xe_send.at[i, ch], recv_sem=xe_recv.at[i, ch],
                    device_id=device(lax.rem(me_s + n - o, n), place), device_id_type=MESH,
                )
                copy.start()
                xe_copies.append(copy)
    for s in range(S):
        for c in range(24):
            guess[pl.ds((s * 24 + c) * T, T), :] = xe0[s, pl.ds(c, T, stride=24), :]

    row = lax.broadcasted_iota(jnp.int32, (1, TP, 128), 1)
    column = lax.rem(lax.broadcasted_iota(jnp.int32, (1, TP, 128), 2), LX)

    def shift(v, d, by):
        if d == 0:
            border = LX - 1 if by > 0 else 0
            inside = pltpu.roll(v, (-by) % 128, 2)
            wrapped = pltpu.roll(v, (by * (LX - 1)) % 128, 2)
            return jnp.where(column == border, wrapped, inside)
        return pltpu.roll(v, (-by * LX) % 128, 2)

    def plane_hops(x, o, acc):
        for d in range(2):
            u = link(o, d)
            ahead = each(project(-1, d, x), lambda v: shift(v, d, 1))
            acc = rebuild(-1, d, color_mul(u, ahead), acc)
            behind = each(color_adj(u, project(1, d, x)), lambda v: shift(v, d, -1))
            acc = rebuild(1, d, behind, acc)
        return acc

    def z_hops(ahead, behind, o, acc):
        acc = rebuild(-1, 2, color_mul(link(o, 2), project(-1, 2, ahead)), acc)
        return rebuild(1, 2, color_adj(link(o - 1, 2), project(1, 2, behind)), acc)

    def t_hops(x, o, hbuf, gbuf, index, acc):
        u = link(o, 3)

        def joined(half, halo, by, at):
            return [
                tuple(
                    jnp.where(row == at, jnp.broadcast_to(q, (3, TP, 128)), pltpu.roll(v, by % TP, 1))
                    for v, q in zip(hv, qv)
                )
                for hv, qv in zip(half, halo)
            ]

        ahead = joined(project(-1, 3, x), get_halo(hbuf, index, top_flip), -1, T - 1)
        acc = rebuild(-1, 3, color_mul(u, ahead), acc)
        behind = joined(
            color_adj(u, project(1, 3, x)), get_halo(gbuf, index, bottom_flip), 1, 0
        )
        return rebuild(1, 3, behind, acc)

    zero = [(jnp.zeros((3, TP, 128), jnp.float32),) * 2] * 4

    def keep(s, acc):
        for sp in range(4):
            for p in range(2):
                acc_ref[s, pl.ds(p * 12 + sp * 3, 3)] = acc[sp][p]

    def kept(s):
        return [
            tuple(acc_ref[s, pl.ds(p * 12 + sp * 3, 3)] for p in range(2)) for sp in range(4)
        ]

    def updated(x, acc, i, s, write):
        rate = slots[s * NT, pl.ds(rows, 1), :]
        for sp in range(4):
            for p in range(2):
                for c in range(3):
                    comp = p * 12 + sp * 3 + c
                    b = sr[i, pl.ds((s * 24 + comp) * T, TP), :]
                    v = x[sp][p][c]
                    write(comp, v + rate * (b - (v - HOPPING * acc[sp][p][c])))

    def slot(offsets, o, s):
        return offsets.index(o % n) * S + s

    def loop(body):
        def step_body(s, carry):
            body(s)
            return carry

        lax.fori_loop(0, S, step_body, 0)

    loop(lambda s: keep(s, plane_hops(tile(xe0, s), 0, zero)))
    for copy in h_copies + g_copies:
        copy.wait_recv()
    loop(lambda s: keep(s, t_hops(tile(xe0, s), 0, hr0, gr0, s, kept(s))))
    for copy in xe_copies:
        copy.wait_recv()
    def first(i, o, s):
        x = tile(xe0, slot(d0, o, s))
        acc = kept(s) if i == 0 else plane_hops(x, o, zero)
        if i:
            acc = t_hops(x, o, hr0, gr0, i * S + s, acc)
        acc = z_hops(tile(xe0, slot(d0, o + 1, s)), tile(xe0, slot(d0, o - 1, s)), o, acc)

        def write(comp, v):
            xe1[i * S + s, pl.ds(comp, TP, stride=24), :] = v

        updated(x, acc, i, s, write)

    loop(lambda s: first(0, 0, s))

    edges_all(xe1, 1)
    h_next = send_halo(hs.at[1], hr1, h1_sem.at[0], h1_sem.at[1], below, [0])
    g_next = send_halo(gs.at[1], gr1, g1_sem.at[0], g1_sem.at[1], above, [0])
    for i in src_copies:
        src_copies[i].wait_recv()
    for i, o in enumerate(d1):
        if o:
            loop(lambda s: first(i, o, s))

    def inner(s):
        x = tile(xe1, s)
        acc = plane_hops(x, 0, zero)
        keep(s, z_hops(tile(xe1, slot(d1, 1, s)), tile(xe1, slot(d1, -1, s)), 0, acc))

    loop(inner)
    for copy in h_next + g_next:
        copy.wait_recv()

    def last(s):
        x = tile(xe1, s)
        acc = t_hops(x, 0, hr1, gr1, s, kept(s))

        def write(comp, v):
            sol[pl.ds((s * 24 + comp) * T, T), :] = v[0:T]

        updated(x, acc, 0, s, write)

    loop(last)
    for copy in sent + xe_copies + h_copies + g_copies + h_next + g_next:
        copy.wait_send()
    pltpu.make_async_copy(every, every, ar_send).wait()


def solution(mesh):
    n, L, U = mesh.shape["src"], mesh.shape["lat"], mesh.shape["sub"]

    def shards(sources, eigvecs, eigvals, links, damping):
        S, _, T, _, _ = sources.shape
        K, LZ = eigvecs.shape[0], links.shape[3]
        TP = -(-T // 8) * 8
        V = T * 24
        N = n * L * U
        rows = 2 * S * K // 128
        d0 = len(distinct((0, 1, -1, 2, -2), n))
        d1 = len(distinct((0, 1, -1), n))
        dl = len(distinct((0, 1, -1, -2), n))
        vmem = pl.BlockSpec(memory_space=pltpu.VMEM)
        hbm = pl.BlockSpec(memory_space=pltpu.HBM)
        f32 = jnp.float32
        dma = pltpu.SemaphoreType.DMA
        chunks = T // 2 if T % 2 == 0 else 1
        guess, result = pl.pallas_call(
            functools.partial(kernel, (T, LZ, S, K, TP), (n, L, U)),
            out_shape=[jax.ShapeDtypeStruct((S * V, 128), f32)] * 2,
            in_specs=[hbm] * 5,
            out_specs=[vmem, vmem],
            scratch_shapes=[
                pltpu.VMEM((S * V, 128), f32),
                pltpu.VMEM((K, V, 128), jnp.bfloat16),
                pltpu.VMEM((1, K), f32),
                pltpu.VMEM((72 * T * LZ, 128), f32),
                pltpu.VMEM((1, 1), f32),
                dma((4,)), dma((K // EIG_BLOCK,)),
                pltpu.VMEM((S, V, 128), f32),
                pltpu.VMEM((S, V, 128), f32),
                pltpu.VMEM((2 * S * K, 128), f32),
                pltpu.VMEM((N, rows + 1, 128), f32),
                pltpu.VMEM((2 * S * K, 128), f32),
                pltpu.VMEM((d0 * S, TP * 24, 128), f32),
                pltpu.VMEM((d1 * S, TP * 24, 128), f32),
                pltpu.VMEM((d1, S * V + 8, 128), f32),
                pltpu.VMEM((dl, 72, TP, 128), f32),
                pltpu.VMEM((2, S, 12, 1, 128), f32),
                pltpu.VMEM((2, S, 12, 1, 128), f32),
                pltpu.VMEM((d1 * S, 12, 1, 128), f32),
                pltpu.VMEM((d1 * S, 12, 1, 128), f32),
                pltpu.VMEM((S, 12, 1, 128), f32),
                pltpu.VMEM((S, 12, 1, 128), f32),
                pltpu.VMEM((S, 24, TP, 128), f32),
                dma, dma, dma((d1,)), dma((d1,)), dma((d0, chunks)), dma((d0, chunks)),
                dma((d1,)), dma((d1,)), dma((d1,)), dma((d1,)), dma((2, 1)), dma((2, 1)),
            ],
            compiler_params=pltpu.CompilerParams(
                collective_id=0, has_side_effects=True, vmem_limit_bytes=63 * 1024 * 1024
            ),
        )(
            sources.reshape(S * V, 128),
            eigvecs.transpose(0, 2, 3, 1, 4).reshape(K, V, 128),
            eigvals.reshape(1, K),
            links.reshape(72 * T * LZ, 128),
            damping.reshape(1, 1),
        )
        return guess.reshape(sources.shape), result.reshape(sources.shape)

    spread = P(None, None, ("lat", "sub"), "src", None)
    return jax.shard_map(
        shards,
        mesh=mesh,
        in_specs=(spread, spread, P(), P(None, None, ("lat", "sub"), None, None), P("src")),
        out_specs=(spread, spread),
        check_vma=False,
    )
```

```python
import functools
import math

import jax
import jax.numpy as jnp
from jax import lax
from jax.experimental import pallas as pl
from jax.experimental.pallas import tpu as pltpu
from jax.sharding import PartitionSpec as P

LX = 16
EIG_BLOCK = 8
HOPPING = 0.12
MESH = pl.DeviceIdType.MESH

BLOCKS = [((1, 1), (0, 1)), ((1, 2), (0, 0)), ((0, 1), (1, 3)), ((0, 0), (1, 0))]
BLOCKS_H = [((1, 3), (0, 3)), ((1, 0), (0, 2)), ((0, 3), (1, 1)), ((0, 0), (1, 0))]


def add_phase(a, b, power):
    power %= 4
    if power == 0:
        return a[0] + b[0], a[1] + b[1]
    if power == 1:
        return a[0] - b[1], a[1] + b[0]
    if power == 2:
        return a[0] - b[0], a[1] - b[1]
    return a[0] + b[1], a[1] - b[0]


def project(sign, d, x):
    turn = 0 if sign > 0 else 2
    return [add_phase(x[r], x[2 + BLOCKS[d][r][0]], BLOCKS[d][r][1] + turn) for r in range(2)]


def rebuild(sign, d, half, acc):
    turn = 0 if sign > 0 else 2
    out = [add_phase(acc[r], half[r], 0) for r in range(2)]
    for r in range(2):
        col, power = BLOCKS_H[d][r]
        out.append(add_phase(acc[2 + r], half[col], power + turn))
    return out


def color_mul(u, half):
    ur, ui = u
    out = []
    for hr, hi in half:
        re = im = None
        for c in range(3):
            a, b = ur[:, c], ui[:, c]
            x, y = hr[c][None], hi[c][None]
            tr, ti = a * x - b * y, a * y + b * x
            re, im = (tr, ti) if re is None else (re + tr, im + ti)
        out.append((re, im))
    return out


def color_adj(u, half):
    ur, ui = u
    out = []
    for hr, hi in half:
        re = im = None
        for c in range(3):
            a, b = ur[c], ui[c]
            x, y = hr[c][None], hi[c][None]
            tr, ti = a * x + b * y, a * y - b * x
            re, im = (tr, ti) if re is None else (re + tr, im + ti)
        out.append((re, im))
    return out


def each(half, fn):
    return [(fn(re), fn(im)) for re, im in half]


def distinct(offsets, n):
    out = []
    for o in offsets:
        if o % n not in out:
            out.append(o % n)
    return out


def kernel(
    shape, sizes,
    src_hbm, eig_hbm, eigvals_hbm, links_hbm, damping_hbm, guess, sol,
    src, eig, eigvals, links, damping, in_sem, eig_sem,
    sa, sb, corr, slots, w2, xe0, xe1, sr, le, hs, gs, hr0, gr0, hr1, gr1, acc_ref,
    ar_send, ar_recv, sr_send, sr_recv, xe_send, xe_recv, h_send, h_recv, g_send, g_recv,
    h1_sem, g1_sem,
):
    T, LZ, S, K, TP = shape
    n, L, U = sizes
    N = n * L * U
    NT = L * U
    V = T * 24
    d0 = distinct((0, 1, -1, 2, -2), n)
    d1 = distinct((0, 1, -1), n)
    dl = distinct((0, 1, -1, -2), n)
    rows = 2 * S * K // 128
    me_s, me_l, me_u = lax.axis_index("src"), lax.axis_index("lat"), lax.axis_index("sub")
    place = me_l * U + me_u
    me = me_s * NT + place

    def device(s_index, t_index):
        return {"src": s_index, "lat": lax.div(t_index, U), "sub": lax.rem(t_index, U)}

    def of(g):
        return device(lax.div(g, NT), lax.rem(g, NT))

    above, below = lax.rem(place + 1, NT), lax.rem(place + NT - 1, NT)
    top_flip = jnp.where(place == NT - 1, -1.0, 1.0).astype(jnp.float32)
    bottom_flip = jnp.where(place == 0, -1.0, 1.0).astype(jnp.float32)

    barrier = pltpu.get_barrier_semaphore()

    def greet(i, carry):
        pl.semaphore_signal(barrier, inc=1, device_id=of(lax.rem(me + i, N)), device_id_type=MESH)
        return carry

    parts = K // EIG_BLOCK
    loads = [
        pltpu.make_async_copy(a, b, in_sem.at[i])
        for i, (a, b) in enumerate(
            [(src_hbm, src), (damping_hbm, damping), (eigvals_hbm, eigvals), (links_hbm, links)]
        )
    ]
    eig_loads = [
        pltpu.make_async_copy(
            eig_hbm.at[pl.ds(j * EIG_BLOCK, EIG_BLOCK)], eig.at[pl.ds(j * EIG_BLOCK, EIG_BLOCK)],
            eig_sem.at[j],
        )
        for j in range(parts)
    ]
    loads[0].start()
    lax.fori_loop(1, N, greet, 0)
    for copy in eig_loads + loads[1:]:
        copy.start()
    loads[0].wait()

    for s in range(S):
        for t in range(T):
            low = [
                src[pl.ds(s * V + p * 12 * T + t, 12, stride=T), :]
                .astype(jnp.bfloat16)
                .astype(jnp.float32)
                for p in range(2)
            ]
            sa[s, pl.ds(t * 24, 12), :] = low[0]
            sa[s, pl.ds(t * 24 + 12, 12), :] = low[1]
            sb[s, pl.ds(t * 24, 12), :] = low[1]
            sb[s, pl.ds(t * 24 + 12, 12), :] = -low[0]

    def correlate(k, carry):
        e = eig[k].astype(jnp.float32)
        for p, ref in enumerate((sa, sb)):
            for s in range(S):
                part = jnp.sum((e * ref[s]).reshape(V // 8, 8, 128), axis=0)
                corr[pl.ds((p * S + s) * K + k, 1), :] = jnp.sum(part, axis=0, keepdims=True)
        return carry

    sr[0, pl.ds(0, S * V), :] = src[...]
    sent = []
    src_copies = {}
    for j in range(parts):
        if j == parts // 2:
            pl.semaphore_wait(barrier, N - 1)
        eig_loads[j].wait()
        lax.fori_loop(j * EIG_BLOCK, (j + 1) * EIG_BLOCK, correlate, 0)
    flat = lax.dot_general(
        jnp.ones((8, 128), jnp.float32), corr[...], (((1,), (1,)), ((), ())),
        preferred_element_type=jnp.float32, precision=lax.Precision.HIGHEST,
    )
    for r in range(rows):
        slots[me, pl.ds(r, 1), :] = flat[0:1, r * 128 : (r + 1) * 128]
    loads[1].wait()
    slots[me, pl.ds(rows, 1), :] = jnp.broadcast_to(damping[...], (1, 128))

    def spread(i, carry):
        pltpu.make_async_remote_copy(
            src_ref=slots.at[me], dst_ref=slots.at[me], send_sem=ar_send, recv_sem=ar_recv,
            device_id=of(lax.rem(me + i, N)), device_id_type=MESH,
        ).start()
        return carry

    lax.fori_loop(1, N, spread, 0)
    for i, o in enumerate(d1):
        if o:
            copy = pltpu.make_async_remote_copy(
                src_ref=src, dst_ref=sr.at[i, pl.ds(0, S * V)],
                send_sem=sr_send.at[i], recv_sem=sr_recv.at[i],
                device_id=device(lax.rem(me_s + n - o, n), place), device_id_type=MESH,
            )
            copy.start()
            sent.append(copy)
            src_copies[i] = copy
    loads[2].wait()
    loads[3].wait()

    for i, o in enumerate(dl):
        z = lax.rem(me_s + o, n)

        def arrange(c, carry):
            le[i, c, pl.ds(0, T), :] = links[pl.ds(c * T * LZ + z, T, stride=LZ), :]
            return carry

        lax.fori_loop(0, 72, arrange, 0)

    every = slots.at[pl.ds(0, N - 1)]
    pltpu.make_async_copy(every, every, ar_recv).wait()
    total = jnp.sum(slots[...], axis=0)
    eye = lax.broadcasted_iota(jnp.int32, (128, 128), 0) == lax.broadcasted_iota(
        jnp.int32, (128, 128), 1
    )
    values = jnp.concatenate([eigvals[...]] * (128 // K), axis=1)
    scale = math.sqrt(24 * T * NT * LZ * 128)
    for r in range(rows):
        w = (total[r : r + 1] / scale / values).astype(jnp.bfloat16).astype(jnp.float32)
        w2[pl.ds(r * 128, 128), :] = jnp.dot(
            jnp.where(eye, w, 0.0).astype(jnp.bfloat16), jnp.ones((128, 128), jnp.bfloat16),
            preferred_element_type=jnp.float32,
        )

    def tile(ref, index):
        parts = [
            [
                jnp.stack([ref[index, pl.ds(p * 12 + sp * 3 + c, TP, stride=24), :] for c in range(3)])
                for sp in range(4)
            ]
            for p in range(2)
        ]
        return [(parts[0][sp], parts[1][sp]) for sp in range(4)]

    def link(o, d):
        i = dl.index(o % n)
        return (
            le[i, pl.ds(d * 18, 9)].reshape(3, 3, TP, 128),
            le[i, pl.ds(d * 18 + 9, 9)].reshape(3, 3, TP, 128),
        )

    def put_halo(buf, s, half, row):
        for p in range(2):
            for sp in range(2):
                buf[s, pl.ds(p * 6 + sp * 3, 3)] = half[sp][p][:, row : row + 1, :]

    def get_halo(buf, index, flip):
        return [
            tuple(buf[index, pl.ds(p * 6 + sp * 3, 3)] * flip for p in range(2)) for sp in range(2)
        ]

    def edges_all(ref, j):
        def body(s, carry):
            x = tile(ref, s)
            put_halo(hs.at[j], s, project(-1, 3, x), 0)
            put_halo(gs.at[j], s, color_adj(link(0, 3), project(1, 3, x)), T - 1)
            return carry

        lax.fori_loop(0, S, body, 0)

    def send_halo(buf, dest, send, recv, t_index, offsets):
        out = []
        for i, o in enumerate(offsets):
            copy = pltpu.make_async_remote_copy(
                src_ref=buf, dst_ref=dest.at[pl.ds(i * S, S)], send_sem=send.at[i],
                recv_sem=recv.at[i], device_id=device(lax.rem(me_s + n - o, n), t_index),
                device_id_type=MESH,
            )
            copy.start()
            out.append(copy)
        return out

    step = 48 if T % 2 == 0 else V
    chunks = list(range(V // step))
    order = [chunks[0]] + chunks[-1:0:-1]
    xe_copies = []
    h_copies = g_copies = None
    for done, ch in enumerate(order):

        def mix(k, acc):
            e = eig[k, pl.ds(ch * step, step), :].astype(jnp.float32)
            return tuple(
                a + w2[pl.ds(j * K + k, 1), :] * e for j, a in enumerate(acc)
            )

        acc = lax.fori_loop(
            0, K, mix, tuple(jnp.zeros((step, 128), jnp.float32) for _ in range(2 * S)), unroll=4
        )
        for s in range(S):
            one, two = acc[s], acc[S + s]
            for t in range(step // 24):
                b = t * 24
                turned = jnp.concatenate([-two[b + 12 : b + 24], two[b : b + 12]], axis=0)
                xe0[s, pl.ds(ch * step + b, 24), :] = one[b : b + 24] + turned
        if done == min(1, len(order) - 1):
            edges_all(xe0, 0)
            h_copies = send_halo(hs.at[0], hr0, h_send, h_recv, below, d1)
            g_copies = send_halo(gs.at[0], gr0, g_send, g_recv, above, d1)
        for i, o in enumerate(d0):
            if o:
                part = pl.ds(ch * step, step)
                copy = pltpu.make_async_remote_copy(
                    src_ref=xe0.at[pl.ds(0, S), part], dst_ref=xe0.at[pl.ds(i * S, S), part],
                    send_sem=xe_send.at[i, ch], recv_sem=xe_recv.at[i, ch],
                    device_id=device(lax.rem(me_s + n - o, n), place), device_id_type=MESH,
                )
                copy.start()
                xe_copies.append(copy)
    for s in range(S):
        for c in range(24):
            guess[pl.ds((s * 24 + c) * T, T), :] = xe0[s, pl.ds(c, T, stride=24), :]

    row = lax.broadcasted_iota(jnp.int32, (1, TP, 128), 1)
    column = lax.rem(lax.broadcasted_iota(jnp.int32, (1, TP, 128), 2), LX)

    def shift(v, d, by):
        if d == 0:
            border = LX - 1 if by > 0 else 0
            inside = pltpu.roll(v, (-by) % 128, 2)
            wrapped = pltpu.roll(v, (by * (LX - 1)) % 128, 2)
            return jnp.where(column == border, wrapped, inside)
        return pltpu.roll(v, (-by * LX) % 128, 2)

    def plane_hops(x, o, acc):
        for d in range(2):
            u = link(o, d)
            ahead = each(project(-1, d, x), lambda v: shift(v, d, 1))
            acc = rebuild(-1, d, color_mul(u, ahead), acc)
            behind = each(color_adj(u, project(1, d, x)), lambda v: shift(v, d, -1))
            acc = rebuild(1, d, behind, acc)
        return acc

    def z_hops(ahead, behind, o, acc):
        acc = rebuild(-1, 2, color_mul(link(o, 2), project(-1, 2, ahead)), acc)
        return rebuild(1, 2, color_adj(link(o - 1, 2), project(1, 2, behind)), acc)

    def t_hops(x, o, hbuf, gbuf, index, acc):
        u = link(o, 3)

        def joined(half, halo, by, at):
            return [
                tuple(
                    jnp.where(row == at, jnp.broadcast_to(q, (3, TP, 128)), pltpu.roll(v, by % TP, 1))
                    for v, q in zip(hv, qv)
                )
                for hv, qv in zip(half, halo)
            ]

        ahead = joined(project(-1, 3, x), get_halo(hbuf, index, top_flip), -1, T - 1)
        acc = rebuild(-1, 3, color_mul(u, ahead), acc)
        behind = joined(
            color_adj(u, project(1, 3, x)), get_halo(gbuf, index, bottom_flip), 1, 0
        )
        return rebuild(1, 3, behind, acc)

    zero = [(jnp.zeros((3, TP, 128), jnp.float32),) * 2] * 4

    def keep(s, acc):
        for sp in range(4):
            for p in range(2):
                acc_ref[s, pl.ds(p * 12 + sp * 3, 3)] = acc[sp][p]

    def kept(s):
        return [
            tuple(acc_ref[s, pl.ds(p * 12 + sp * 3, 3)] for p in range(2)) for sp in range(4)
        ]

    def updated(x, acc, i, s, write):
        rate = slots[s * NT, pl.ds(rows, 1), :]
        for sp in range(4):
            for p in range(2):
                for c in range(3):
                    comp = p * 12 + sp * 3 + c
                    b = sr[i, pl.ds((s * 24 + comp) * T, TP), :]
                    v = x[sp][p][c]
                    write(comp, v + rate * (b - (v - HOPPING * acc[sp][p][c])))

    def slot(offsets, o, s):
        return offsets.index(o % n) * S + s

    def loop(body):
        def step_body(s, carry):
            body(s)
            return carry

        lax.fori_loop(0, S, step_body, 0)

    loop(lambda s: keep(s, plane_hops(tile(xe0, s), 0, zero)))
    for copy in h_copies + g_copies:
        copy.wait_recv()
    loop(lambda s: keep(s, t_hops(tile(xe0, s), 0, hr0, gr0, s, kept(s))))
    for copy in xe_copies:
        copy.wait_recv()
    def first(i, o, s):
        x = tile(xe0, slot(d0, o, s))
        acc = kept(s) if i == 0 else plane_hops(x, o, zero)
        if i:
            acc = t_hops(x, o, hr0, gr0, i * S + s, acc)
        acc = z_hops(tile(xe0, slot(d0, o + 1, s)), tile(xe0, slot(d0, o - 1, s)), o, acc)

        def write(comp, v):
            xe1[i * S + s, pl.ds(comp, TP, stride=24), :] = v

        updated(x, acc, i, s, write)

    loop(lambda s: first(0, 0, s))

    edges_all(xe1, 1)
    h_next = send_halo(hs.at[1], hr1, h1_sem.at[0], h1_sem.at[1], below, [0])
    g_next = send_halo(gs.at[1], gr1, g1_sem.at[0], g1_sem.at[1], above, [0])
    for i in src_copies:
        src_copies[i].wait_recv()
    for i, o in enumerate(d1):
        if o:
            loop(lambda s: first(i, o, s))

    def inner(s):
        x = tile(xe1, s)
        acc = plane_hops(x, 0, zero)
        keep(s, z_hops(tile(xe1, slot(d1, 1, s)), tile(xe1, slot(d1, -1, s)), 0, acc))

    loop(inner)
    for copy in h_next + g_next:
        copy.wait_recv()

    def last(s):
        x = tile(xe1, s)
        acc = t_hops(x, 0, hr1, gr1, s, kept(s))

        def write(comp, v):
            sol[pl.ds((s * 24 + comp) * T, T), :] = v[0:T]

        updated(x, acc, 0, s, write)

    loop(last)
    for copy in sent + xe_copies + h_copies + g_copies + h_next + g_next:
        copy.wait_send()
    pltpu.make_async_copy(every, every, ar_send).wait()


def solution(mesh):
    n, L, U = mesh.shape["src"], mesh.shape["lat"], mesh.shape["sub"]

    def shards(sources, eigvecs, eigvals, links, damping):
        S, _, T, _, _ = sources.shape
        K, LZ = eigvecs.shape[0], links.shape[3]
        TP = -(-T // 8) * 8
        V = T * 24
        N = n * L * U
        rows = 2 * S * K // 128
        d0 = len(distinct((0, 1, -1, 2, -2), n))
        d1 = len(distinct((0, 1, -1), n))
        dl = len(distinct((0, 1, -1, -2), n))
        vmem = pl.BlockSpec(memory_space=pltpu.VMEM)
        hbm = pl.BlockSpec(memory_space=pltpu.HBM)
        f32 = jnp.float32
        dma = pltpu.SemaphoreType.DMA
        chunks = T // 2 if T % 2 == 0 else 1
        guess, result = pl.pallas_call(
            functools.partial(kernel, (T, LZ, S, K, TP), (n, L, U)),
            out_shape=[pltpu.VMEM((S * V, 128), f32)] * 2,
            in_specs=[hbm] * 5,
            out_specs=[vmem, vmem],
            scratch_shapes=[
                pltpu.VMEM((S * V, 128), f32),
                pltpu.VMEM((K, V, 128), jnp.bfloat16),
                pltpu.VMEM((1, K), f32),
                pltpu.VMEM((72 * T * LZ, 128), f32),
                pltpu.VMEM((1, 1), f32),
                dma((4,)), dma((K // EIG_BLOCK,)),
                pltpu.VMEM((S, V, 128), f32),
                pltpu.VMEM((S, V, 128), f32),
                pltpu.VMEM((2 * S * K, 128), f32),
                pltpu.VMEM((N, rows + 1, 128), f32),
                pltpu.VMEM((2 * S * K, 128), f32),
                pltpu.VMEM((d0 * S, TP * 24, 128), f32),
                pltpu.VMEM((d1 * S, TP * 24, 128), f32),
                pltpu.VMEM((d1, S * V + 8, 128), f32),
                pltpu.VMEM((dl, 72, TP, 128), f32),
                pltpu.VMEM((2, S, 12, 1, 128), f32),
                pltpu.VMEM((2, S, 12, 1, 128), f32),
                pltpu.VMEM((d1 * S, 12, 1, 128), f32),
                pltpu.VMEM((d1 * S, 12, 1, 128), f32),
                pltpu.VMEM((S, 12, 1, 128), f32),
                pltpu.VMEM((S, 12, 1, 128), f32),
                pltpu.VMEM((S, 24, TP, 128), f32),
                dma, dma, dma((d1,)), dma((d1,)), dma((d0, chunks)), dma((d0, chunks)),
                dma((d1,)), dma((d1,)), dma((d1,)), dma((d1,)), dma((2, 1)), dma((2, 1)),
            ],
            compiler_params=pltpu.CompilerParams(
                collective_id=0, has_side_effects=True, vmem_limit_bytes=61000 * 1024
            ),
        )(
            sources.reshape(S * V, 128),
            eigvecs.transpose(0, 2, 3, 1, 4).reshape(K, V, 128),
            eigvals.reshape(1, K),
            links.reshape(72 * T * LZ, 128),
            damping.reshape(1, 1),
        )
        return guess.reshape(sources.shape), result.reshape(sources.shape)

    spread = P(None, None, ("lat", "sub"), "src", None)
    return jax.shard_map(
        shards,
        mesh=mesh,
        in_specs=(spread, spread, P(), P(None, None, ("lat", "sub"), None, None), P("src")),
        out_specs=(spread, spread),
        check_vma=False,
    )
```

```python
import functools
import math

import jax
import jax.numpy as jnp
from jax import lax
from jax.experimental import pallas as pl
from jax.experimental.pallas import tpu as pltpu
from jax.sharding import PartitionSpec as P

LX = 16
EIG_BLOCK = 8
HOPPING = 0.12
MESH = pl.DeviceIdType.MESH

BLOCKS = [((1, 1), (0, 1)), ((1, 2), (0, 0)), ((0, 1), (1, 3)), ((0, 0), (1, 0))]
BLOCKS_H = [((1, 3), (0, 3)), ((1, 0), (0, 2)), ((0, 3), (1, 1)), ((0, 0), (1, 0))]


def add_phase(a, b, power):
    power %= 4
    if power == 0:
        return a[0] + b[0], a[1] + b[1]
    if power == 1:
        return a[0] - b[1], a[1] + b[0]
    if power == 2:
        return a[0] - b[0], a[1] - b[1]
    return a[0] + b[1], a[1] - b[0]


def project(sign, d, x):
    turn = 0 if sign > 0 else 2
    return [add_phase(x[r], x[2 + BLOCKS[d][r][0]], BLOCKS[d][r][1] + turn) for r in range(2)]


def rebuild(sign, d, half, acc):
    turn = 0 if sign > 0 else 2
    out = [add_phase(acc[r], half[r], 0) for r in range(2)]
    for r in range(2):
        col, power = BLOCKS_H[d][r]
        out.append(add_phase(acc[2 + r], half[col], power + turn))
    return out


def color_mul(u, half):
    ur, ui = u
    out = []
    for hr, hi in half:
        re = im = None
        for c in range(3):
            a, b = ur[:, c], ui[:, c]
            x, y = hr[c][None], hi[c][None]
            tr, ti = a * x - b * y, a * y + b * x
            re, im = (tr, ti) if re is None else (re + tr, im + ti)
        out.append((re, im))
    return out


def color_adj(u, half):
    ur, ui = u
    out = []
    for hr, hi in half:
        re = im = None
        for c in range(3):
            a, b = ur[c], ui[c]
            x, y = hr[c][None], hi[c][None]
            tr, ti = a * x + b * y, a * y - b * x
            re, im = (tr, ti) if re is None else (re + tr, im + ti)
        out.append((re, im))
    return out


def each(half, fn):
    return [(fn(re), fn(im)) for re, im in half]


def distinct(offsets, n):
    out = []
    for o in offsets:
        if o % n not in out:
            out.append(o % n)
    return out


def kernel(
    shape, sizes,
    src_hbm, eig_hbm, eigvals_hbm, links_hbm, damping_hbm, guess, sol,
    src, eig, eigvals, links, damping, in_sem, eig_sem,
    sa, sb, corr, slots, w2, xe0, xe1, sr, le, hs, gs, hr0, gr0, hr1, gr1, acc_ref,
    ar_send, ar_recv, sr_send, sr_recv, xe_send, xe_recv, h_send, h_recv, g_send, g_recv,
    h1_sem, g1_sem,
):
    T, LZ, S, K, TP = shape
    n, L, U = sizes
    N = n * L * U
    NT = L * U
    V = T * 24
    d0 = distinct((0, 1, -1, 2, -2), n)
    d1 = distinct((0, 1, -1), n)
    dl = distinct((0, 1, -1, -2), n)
    rows = 2 * S * K // 128
    me_s, me_l, me_u = lax.axis_index("src"), lax.axis_index("lat"), lax.axis_index("sub")
    place = me_l * U + me_u
    me = me_s * NT + place

    def device(s_index, t_index):
        return {"src": s_index, "lat": lax.div(t_index, U), "sub": lax.rem(t_index, U)}

    def of(g):
        return device(lax.div(g, NT), lax.rem(g, NT))

    above, below = lax.rem(place + 1, NT), lax.rem(place + NT - 1, NT)
    top_flip = jnp.where(place == NT - 1, -1.0, 1.0).astype(jnp.float32)
    bottom_flip = jnp.where(place == 0, -1.0, 1.0).astype(jnp.float32)

    barrier = pltpu.get_barrier_semaphore()

    def greet(i, carry):
        pl.semaphore_signal(barrier, inc=1, device_id=of(lax.rem(me + i, N)), device_id_type=MESH)
        return carry

    parts = K // EIG_BLOCK
    loads = [
        pltpu.make_async_copy(a, b, in_sem.at[i])
        for i, (a, b) in enumerate(
            [(src_hbm, src), (damping_hbm, damping), (eigvals_hbm, eigvals), (links_hbm, links)]
        )
    ]
    eig_loads = [
        pltpu.make_async_copy(
            eig_hbm.at[pl.ds(j * EIG_BLOCK, EIG_BLOCK)], eig.at[pl.ds(j * EIG_BLOCK, EIG_BLOCK)],
            eig_sem.at[j],
        )
        for j in range(parts)
    ]
    loads[0].start()
    lax.fori_loop(1, N, greet, 0)
    for copy in eig_loads + loads[1:]:
        copy.start()
    loads[0].wait()

    for s in range(S):
        for t in range(T):
            low = [
                src[pl.ds(s * V + p * 12 * T + t, 12, stride=T), :]
                .astype(jnp.bfloat16)
                .astype(jnp.float32)
                for p in range(2)
            ]
            sa[s, pl.ds(t * 24, 12), :] = low[0]
            sa[s, pl.ds(t * 24 + 12, 12), :] = low[1]
            sb[s, pl.ds(t * 24, 12), :] = low[1]
            sb[s, pl.ds(t * 24 + 12, 12), :] = -low[0]

    def correlate(k, carry):
        e = eig[k].astype(jnp.float32)
        for p, ref in enumerate((sa, sb)):
            for s in range(S):
                part = jnp.sum((e * ref[s]).reshape(V // 8, 8, 128), axis=0)
                corr[pl.ds((p * S + s) * K + k, 1), :] = jnp.sum(part, axis=0, keepdims=True)
        return carry

    sr[0, pl.ds(0, S * V), :] = src[...]
    sent = []
    src_copies = {}
    for j in range(parts):
        if j == parts // 2:
            pl.semaphore_wait(barrier, N - 1)
        eig_loads[j].wait()
        lax.fori_loop(j * EIG_BLOCK, (j + 1) * EIG_BLOCK, correlate, 0, unroll=4)
    flat = lax.dot_general(
        jnp.ones((8, 128), jnp.float32), corr[...], (((1,), (1,)), ((), ())),
        preferred_element_type=jnp.float32, precision=lax.Precision.HIGHEST,
    )
    for r in range(rows):
        slots[me, pl.ds(r, 1), :] = flat[0:1, r * 128 : (r + 1) * 128]
    loads[1].wait()
    slots[me, pl.ds(rows, 1), :] = jnp.broadcast_to(damping[...], (1, 128))

    def spread(i, carry):
        pltpu.make_async_remote_copy(
            src_ref=slots.at[me], dst_ref=slots.at[me], send_sem=ar_send, recv_sem=ar_recv,
            device_id=of(lax.rem(me + i, N)), device_id_type=MESH,
        ).start()
        return carry

    lax.fori_loop(1, N, spread, 0)
    for i, o in enumerate(d1):
        if o:
            copy = pltpu.make_async_remote_copy(
                src_ref=src, dst_ref=sr.at[i, pl.ds(0, S * V)],
                send_sem=sr_send.at[i], recv_sem=sr_recv.at[i],
                device_id=device(lax.rem(me_s + n - o, n), place), device_id_type=MESH,
            )
            copy.start()
            sent.append(copy)
            src_copies[i] = copy
    loads[2].wait()
    loads[3].wait()

    for i, o in enumerate(dl):
        z = lax.rem(me_s + o, n)

        def arrange(c, carry):
            le[i, c, pl.ds(0, T), :] = links[pl.ds(c * T * LZ + z, T, stride=LZ), :]
            return carry

        lax.fori_loop(0, 72, arrange, 0)

    every = slots.at[pl.ds(0, N - 1)]
    pltpu.make_async_copy(every, every, ar_recv).wait()
    total = jnp.sum(slots[...], axis=0)
    eye = lax.broadcasted_iota(jnp.int32, (128, 128), 0) == lax.broadcasted_iota(
        jnp.int32, (128, 128), 1
    )
    values = jnp.concatenate([eigvals[...]] * (128 // K), axis=1)
    scale = math.sqrt(24 * T * NT * LZ * 128)
    for r in range(rows):
        w = (total[r : r + 1] / scale / values).astype(jnp.bfloat16).astype(jnp.float32)
        w2[pl.ds(r * 128, 128), :] = jnp.dot(
            jnp.where(eye, w, 0.0).astype(jnp.bfloat16), jnp.ones((128, 128), jnp.bfloat16),
            preferred_element_type=jnp.float32,
        )

    def tile(ref, index):
        parts = [
            [
                jnp.stack([ref[index, pl.ds(p * 12 + sp * 3 + c, TP, stride=24), :] for c in range(3)])
                for sp in range(4)
            ]
            for p in range(2)
        ]
        return [(parts[0][sp], parts[1][sp]) for sp in range(4)]

    def link(o, d):
        i = dl.index(o % n)
        return (
            le[i, pl.ds(d * 18, 9)].reshape(3, 3, TP, 128),
            le[i, pl.ds(d * 18 + 9, 9)].reshape(3, 3, TP, 128),
        )

    def put_halo(buf, s, half, row):
        for p in range(2):
            for sp in range(2):
                buf[s, pl.ds(p * 6 + sp * 3, 3)] = half[sp][p][:, row : row + 1, :]

    def get_halo(buf, index, flip):
        return [
            tuple(buf[index, pl.ds(p * 6 + sp * 3, 3)] * flip for p in range(2)) for sp in range(2)
        ]

    def edges_all(ref, j):
        def body(s, carry):
            x = tile(ref, s)
            put_halo(hs.at[j], s, project(-1, 3, x), 0)
            put_halo(gs.at[j], s, color_adj(link(0, 3), project(1, 3, x)), T - 1)
            return carry

        lax.fori_loop(0, S, body, 0)

    def send_halo(buf, dest, send, recv, t_index, offsets):
        out = []
        for i, o in enumerate(offsets):
            copy = pltpu.make_async_remote_copy(
                src_ref=buf, dst_ref=dest.at[pl.ds(i * S, S)], send_sem=send.at[i],
                recv_sem=recv.at[i], device_id=device(lax.rem(me_s + n - o, n), t_index),
                device_id_type=MESH,
            )
            copy.start()
            out.append(copy)
        return out

    step = 48 if T % 2 == 0 else V
    chunks = list(range(V // step))
    order = [chunks[0]] + chunks[-1:0:-1]
    xe_copies = []
    h_copies = g_copies = None
    for done, ch in enumerate(order):

        def mix(k, acc):
            e = eig[k, pl.ds(ch * step, step), :].astype(jnp.float32)
            return tuple(
                a + w2[pl.ds(j * K + k, 1), :] * e for j, a in enumerate(acc)
            )

        acc = lax.fori_loop(
            0, K, mix, tuple(jnp.zeros((step, 128), jnp.float32) for _ in range(2 * S)), unroll=8
        )
        for s in range(S):
            one, two = acc[s], acc[S + s]
            for t in range(step // 24):
                b = t * 24
                turned = jnp.concatenate([-two[b + 12 : b + 24], two[b : b + 12]], axis=0)
                xe0[s, pl.ds(ch * step + b, 24), :] = one[b : b + 24] + turned
        if done == min(1, len(order) - 1):
            edges_all(xe0, 0)
            h_copies = send_halo(hs.at[0], hr0, h_send, h_recv, below, d1)
            g_copies = send_halo(gs.at[0], gr0, g_send, g_recv, above, d1)
        for i, o in enumerate(d0):
            if o:
                part = pl.ds(ch * step, step)
                copy = pltpu.make_async_remote_copy(
                    src_ref=xe0.at[pl.ds(0, S), part], dst_ref=xe0.at[pl.ds(i * S, S), part],
                    send_sem=xe_send.at[i, ch], recv_sem=xe_recv.at[i, ch],
                    device_id=device(lax.rem(me_s + n - o, n), place), device_id_type=MESH,
                )
                copy.start()
                xe_copies.append(copy)
    for s in range(S):
        for c in range(24):
            guess[pl.ds((s * 24 + c) * T, T), :] = xe0[s, pl.ds(c, T, stride=24), :]

    row = lax.broadcasted_iota(jnp.int32, (1, TP, 128), 1)
    column = lax.rem(lax.broadcasted_iota(jnp.int32, (1, TP, 128), 2), LX)

    def shift(v, d, by):
        if d == 0:
            border = LX - 1 if by > 0 else 0
            inside = pltpu.roll(v, (-by) % 128, 2)
            wrapped = pltpu.roll(v, (by * (LX - 1)) % 128, 2)
            return jnp.where(column == border, wrapped, inside)
        return pltpu.roll(v, (-by * LX) % 128, 2)

    def plane_hops(x, o, acc):
        for d in range(2):
            u = link(o, d)
            ahead = each(project(-1, d, x), lambda v: shift(v, d, 1))
            acc = rebuild(-1, d, color_mul(u, ahead), acc)
            behind = each(color_adj(u, project(1, d, x)), lambda v: shift(v, d, -1))
            acc = rebuild(1, d, behind, acc)
        return acc

    def z_hops(ahead, behind, o, acc):
        acc = rebuild(-1, 2, color_mul(link(o, 2), project(-1, 2, ahead)), acc)
        return rebuild(1, 2, color_adj(link(o - 1, 2), project(1, 2, behind)), acc)

    def t_hops(x, o, hbuf, gbuf, index, acc):
        u = link(o, 3)

        def joined(half, halo, by, at):
            return [
                tuple(
                    jnp.where(row == at, jnp.broadcast_to(q, (3, TP, 128)), pltpu.roll(v, by % TP, 1))
                    for v, q in zip(hv, qv)
                )
                for hv, qv in zip(half, halo)
            ]

        ahead = joined(project(-1, 3, x), get_halo(hbuf, index, top_flip), -1, T - 1)
        acc = rebuild(-1, 3, color_mul(u, ahead), acc)
        behind = joined(
            color_adj(u, project(1, 3, x)), get_halo(gbuf, index, bottom_flip), 1, 0
        )
        return rebuild(1, 3, behind, acc)

    zero = [(jnp.zeros((3, TP, 128), jnp.float32),) * 2] * 4

    def keep(s, acc):
        for sp in range(4):
            for p in range(2):
                acc_ref[s, pl.ds(p * 12 + sp * 3, 3)] = acc[sp][p]

    def kept(s):
        return [
            tuple(acc_ref[s, pl.ds(p * 12 + sp * 3, 3)] for p in range(2)) for sp in range(4)
        ]

    def updated(x, acc, i, s, write):
        rate = slots[s * NT, pl.ds(rows, 1), :]
        for sp in range(4):
            for p in range(2):
                for c in range(3):
                    comp = p * 12 + sp * 3 + c
                    b = sr[i, pl.ds((s * 24 + comp) * T, TP), :]
                    v = x[sp][p][c]
                    write(comp, v + rate * (b - (v - HOPPING * acc[sp][p][c])))

    def slot(offsets, o, s):
        return offsets.index(o % n) * S + s

    def loop(body):
        def step_body(s, carry):
            body(s)
            return carry

        lax.fori_loop(0, S, step_body, 0)

    loop(lambda s: keep(s, plane_hops(tile(xe0, s), 0, zero)))
    for copy in h_copies + g_copies:
        copy.wait_recv()
    loop(lambda s: keep(s, t_hops(tile(xe0, s), 0, hr0, gr0, s, kept(s))))
    for copy in xe_copies:
        copy.wait_recv()
    def first(i, o, s):
        x = tile(xe0, slot(d0, o, s))
        acc = kept(s) if i == 0 else plane_hops(x, o, zero)
        if i:
            acc = t_hops(x, o, hr0, gr0, i * S + s, acc)
        acc = z_hops(tile(xe0, slot(d0, o + 1, s)), tile(xe0, slot(d0, o - 1, s)), o, acc)

        def write(comp, v):
            xe1[i * S + s, pl.ds(comp, TP, stride=24), :] = v

        updated(x, acc, i, s, write)

    loop(lambda s: first(0, 0, s))

    edges_all(xe1, 1)
    h_next = send_halo(hs.at[1], hr1, h1_sem.at[0], h1_sem.at[1], below, [0])
    g_next = send_halo(gs.at[1], gr1, g1_sem.at[0], g1_sem.at[1], above, [0])
    for i in src_copies:
        src_copies[i].wait_recv()
    for i, o in enumerate(d1):
        if o:
            loop(lambda s: first(i, o, s))

    def inner(s):
        x = tile(xe1, s)
        acc = plane_hops(x, 0, zero)
        keep(s, z_hops(tile(xe1, slot(d1, 1, s)), tile(xe1, slot(d1, -1, s)), 0, acc))

    loop(inner)
    for copy in h_next + g_next:
        copy.wait_recv()

    def last(s):
        x = tile(xe1, s)
        acc = t_hops(x, 0, hr1, gr1, s, kept(s))

        def write(comp, v):
            sol[pl.ds((s * 24 + comp) * T, T), :] = v[0:T]

        updated(x, acc, 0, s, write)

    loop(last)
    for copy in sent + xe_copies + h_copies + g_copies + h_next + g_next:
        copy.wait_send()
    pltpu.make_async_copy(every, every, ar_send).wait()


def solution(mesh):
    n, L, U = mesh.shape["src"], mesh.shape["lat"], mesh.shape["sub"]

    def shards(sources, eigvecs, eigvals, links, damping):
        S, _, T, _, _ = sources.shape
        K, LZ = eigvecs.shape[0], links.shape[3]
        TP = -(-T // 8) * 8
        V = T * 24
        N = n * L * U
        rows = 2 * S * K // 128
        d0 = len(distinct((0, 1, -1, 2, -2), n))
        d1 = len(distinct((0, 1, -1), n))
        dl = len(distinct((0, 1, -1, -2), n))
        vmem = pl.BlockSpec(memory_space=pltpu.VMEM)
        hbm = pl.BlockSpec(memory_space=pltpu.HBM)
        f32 = jnp.float32
        dma = pltpu.SemaphoreType.DMA
        chunks = T // 2 if T % 2 == 0 else 1
        guess, result = pl.pallas_call(
            functools.partial(kernel, (T, LZ, S, K, TP), (n, L, U)),
            out_shape=[pltpu.VMEM((S * V, 128), f32)] * 2,
            in_specs=[hbm] * 5,
            out_specs=[vmem, vmem],
            scratch_shapes=[
                pltpu.VMEM((S * V, 128), f32),
                pltpu.VMEM((K, V, 128), jnp.bfloat16),
                pltpu.VMEM((1, K), f32),
                pltpu.VMEM((72 * T * LZ, 128), f32),
                pltpu.VMEM((1, 1), f32),
                dma((4,)), dma((K // EIG_BLOCK,)),
                pltpu.VMEM((S, V, 128), f32),
                pltpu.VMEM((S, V, 128), f32),
                pltpu.VMEM((2 * S * K, 128), f32),
                pltpu.VMEM((N, rows + 1, 128), f32),
                pltpu.VMEM((2 * S * K, 128), f32),
                pltpu.VMEM((d0 * S, TP * 24, 128), f32),
                pltpu.VMEM((d1 * S, TP * 24, 128), f32),
                pltpu.VMEM((d1, S * V + 8, 128), f32),
                pltpu.VMEM((dl, 72, TP, 128), f32),
                pltpu.VMEM((2, S, 12, 1, 128), f32),
                pltpu.VMEM((2, S, 12, 1, 128), f32),
                pltpu.VMEM((d1 * S, 12, 1, 128), f32),
                pltpu.VMEM((d1 * S, 12, 1, 128), f32),
                pltpu.VMEM((S, 12, 1, 128), f32),
                pltpu.VMEM((S, 12, 1, 128), f32),
                pltpu.VMEM((S, 24, TP, 128), f32),
                dma, dma, dma((d1,)), dma((d1,)), dma((d0, chunks)), dma((d0, chunks)),
                dma((d1,)), dma((d1,)), dma((d1,)), dma((d1,)), dma((2, 1)), dma((2, 1)),
            ],
            compiler_params=pltpu.CompilerParams(
                collective_id=0, has_side_effects=True, vmem_limit_bytes=61000 * 1024
            ),
        )(
            sources.reshape(S * V, 128),
            eigvecs.transpose(0, 2, 3, 1, 4).reshape(K, V, 128),
            eigvals.reshape(1, K),
            links.reshape(72 * T * LZ, 128),
            damping.reshape(1, 1),
        )
        return guess.reshape(sources.shape), result.reshape(sources.shape)

    spread = P(None, None, ("lat", "sub"), "src", None)
    return jax.shard_map(
        shards,
        mesh=mesh,
        in_specs=(spread, spread, P(), P(None, None, ("lat", "sub"), None, None), P("src")),
        out_specs=(spread, spread),
        check_vma=False,
    )
```
